1024 devices in a mesh: dp: 8 (over x), expert: 64 (over z, y), mp: 2 (over core).
Axes of the slice: x: 8, y: 8, z: 8, core: 2. Of those that a mesh axis runs over, the one named last changes fastest.
Arguments:
- image_rows: bfloat16 [81920, 2048], P(('dp', 'expert', 'mp')), may hold values from -6 to 6
- image_counts: int32 [1024, 16], P(('dp', 'expert', 'mp')), may hold values from 1 to 8, 80 in all within a row
- image_owner: int32 [1024, 16], P(('dp', 'expert', 'mp')), may hold values from 0 to 15, each once within a row
- routes: int32 [131072, 2], P(('dp', 'expert', 'mp')), may hold values from 0 to 63, all different within a row; in each aligned block of 128 rows (0 to 127, 128 to 255, ...) at most 6 rows name the same one
- route_scale: float32 [131072, 2], P(('dp', 'expert', 'mp')), may hold values from 0.1 to 1
- w_gate: bfloat16 [64, 2048, 768], P('expert', None, 'mp'), may hold values from -0.125 to 0.125
- w_up: bfloat16 [64, 2048, 768], P('expert', None, 'mp'), may hold values from -0.125 to 0.125
- w_down: bfloat16 [64, 768, 2048], P('expert', 'mp'), may hold values from -0.21875 to 0.21875
Outputs:
- combined: bfloat16 [131072, 2048], P(('dp', 'expert', 'mp'))
The draws below stay inside these ranges and needn't reach their ends.
Inputs may be any that keep to these rules, and one draw needn't show every extreme that they name: `image_counts`: the counts of each device's images sum to 80, and each count is at most 8, reached on every device. `image_owner`: each device places its 16 images at distinct owners, one each. `routes`: a row's 2 experts are distinct; among the 128 rows of one device no expert is named more than 6 times, and this most is reached on some devices.
All inputs are finite; a program needn't handle non-finite values.
Results may differ from the reference program's by a relative error of at most 0.012.
Values may be sent and summed in bfloat16 or wider, within the bound.
No kernel may reach another device: no remote copies, remote signals or barrier semaphores. Data moves between devices by JAX's collectives and lax.ppermute only.
A program may use at most 64 MiB of HBM per device.

```python
import math
import jax
import jax.numpy as jnp
import numpy as np
from jax import lax

D = 2048
H = 768
TOP = 2
SEQ = 128
OWNERS = 16
SLOT = 8
IMG_ROWS = 80
EXPERTS = 64
CAP_EXP = 6
N_DP = 8
N_EXPERT = 64
N_MP = 2
DEVICES = 1024


def steps_of(key, shape, shards, smallest, high):
    loudness, own = 1.0, jax.random.fold_in(key, 6)
    for axis_at, parts in shards:
        steps = jnp.exp(jax.random.uniform(jax.random.fold_in(own, axis_at), (parts,), jnp.float32, smallest / len(shards), high / len(shards)))
        loudness = loudness * jnp.repeat(steps, shape[axis_at] // parts).reshape([-1 if axis == axis_at else 1 for axis in range(len(shape))])
    return loudness


def split_up(number_of, total, most, skew):
    loads = [(1 << 20) // math.isqrt(grade ** skew) + 1 for grade in range(2, number_of + 1)]
    surplus, given = total - most - (number_of - 1), [1] * (number_of - 1)
    while surplus > 0:
        free = [i for i in range(number_of - 1) if given[i] < most]
        pool, budget = sum([loads[i] for i in free]), surplus
        for i in free:
            addition = min(most - given[i], max(1, budget * loads[i] // pool), surplus)
            given[i] = given[i] + addition
            surplus = surplus - addition
    return np.array([most] + given)


def uneven_parts(stream_key, amount, total, reach, lean):
    if amount == 2:
        one = jax.random.randint(stream_key, (), max(1, total - reach), min(reach, total - 1) + 1)
        return jnp.stack([one, total - one])
    tallies = jnp.asarray(split_up(amount, total, reach, lean), jnp.int32)
    pairs = (amount - 1) // 2
    source_of, taker = tallies[1:1 + 2 * pairs:2], tallies[2:2 + 2 * pairs:2]
    slack = jnp.minimum(source_of - 1, reach - taker)
    moved = jax.random.randint(jax.random.fold_in(stream_key, 1), (pairs,), 0, 1 << 20) % (slack + 1)
    tallies = tallies.at[1:1 + 2 * pairs:2].set(source_of - moved).at[2:2 + 2 * pairs:2].set(taker + moved)
    return tallies[jax.random.permutation(jax.random.fold_in(stream_key, 2), amount)]


def deal_out(stream_key, own, number, rows, amount, top, reach, lean):
    order = jax.random.permutation(stream_key, amount)
    heavy_load, ordinary = load_shares(amount, rows * top, reach, lean, True), load_shares(amount, rows * top, reach, lean, False)
    places = jnp.arange(amount)

    def named(sizes, turn):
        used = int((sizes > 0).sum())
        fixed = max(1, used // 4)
        shifted = fixed + (places - fixed + turn * (used - fixed)) % max(1, amount - fixed)
        return jnp.zeros((amount,), jnp.int32).at[order[jnp.where(places < fixed, places, shifted)]].set(jnp.asarray(sizes, jnp.int32))

    sizes = jnp.where(number % 4 == 0, named(heavy_load, number // 4), named(ordinary, number - number // 4 - 1))
    mixed = jax.random.permutation(jax.random.fold_in(own, 3), amount)
    source_of, taker = mixed[0:amount // 2 * 2:2], mixed[1:amount // 2 * 2:2]
    slack = jnp.minimum(sizes[source_of] - 1, reach - sizes[taker]) // 2
    slack = jnp.where((source_of == order[0]) | (taker == order[0]) | (sizes[taker] == 0), 0, jnp.maximum(slack, 0))
    shifted = jax.random.randint(jax.random.fold_in(own, 4), (amount // 2,), 0, 1 << 20) % (slack + 1)
    sizes = sizes.at[source_of].add(-shifted).at[taker].add(shifted)
    members = jnp.searchsorted(jnp.cumsum(sizes), jnp.arange(rows * top), side="right").astype(jnp.int32)
    table = members.reshape(top, rows).T
    table = table[jax.random.permutation(jax.random.fold_in(own, 1), rows)]
    turn = jax.random.randint(jax.random.fold_in(own, 2), (rows, 1), 0, top)
    return jnp.take_along_axis(table, (jnp.arange(top)[None, :] + turn) % top, axis=1)


def load_shares(count, total, most, slope, full):
    weights = [(1 << 20) // math.isqrt(rank ** slope) + 1 for rank in range(1, count + 1)]
    largest = most if full else min(most, max(-(-total // count), total * weights[0] // sum(weights)))
    least = 1 if total - largest >= count - 1 else 0
    given, surplus = [largest] + [least] * (count - 1), total - largest - least * (count - 1)
    while surplus > 0:
        movable = [i for i in range(1, count) if given[i] < largest] or [i for i in range(1, count) if given[i] < most]
        mass, budget = sum([weights[i] for i in movable]), surplus
        for i in movable:
            more = min(most - given[i], max(1, budget * weights[i] // mass), surplus)
            given[i] = given[i] + more
            surplus = surplus - more
    return np.array(given)


def scatter_about(rng, shape, spread, limit, split=(), kind=jnp.bfloat16):
    array = jax.random.normal(rng, shape, jnp.float32) * spread
    if len(split) > 0:
        array = steps_of(rng, shape, split, -0.22, 0.18) * array
    return jnp.clip(array, min=-limit, max=limit).astype(kind)


def setup_inputs(seed: int = 0) -> dict:
    seeds = jax.random.split(jax.random.key(seed), 9)
    image_rows = scatter_about(seeds[0], (DEVICES * IMG_ROWS, D), 1.0, 6.0, ((0, 1024),))
    image_counts = jax.vmap(lambda own: uneven_parts(own, OWNERS, IMG_ROWS, SLOT, 2))(jax.random.split(seeds[1], DEVICES)).reshape((DEVICES, OWNERS)).astype(jnp.int32)
    image_owner = jax.vmap(lambda own: jax.random.permutation(own, OWNERS))(jax.random.split(seeds[2], DEVICES)).reshape((DEVICES, OWNERS)).astype(jnp.int32)
    routes_keys = jax.random.split(jax.random.fold_in(seeds[3], 1), (DEVICES * SEQ) // SEQ)
    routes_turns = jax.random.permutation(jax.random.fold_in(seeds[3], 3), (DEVICES * SEQ) // SEQ)
    routes = jax.vmap(lambda own, number: deal_out(jax.random.fold_in(seeds[3], 2), own, number, SEQ, EXPERTS, TOP, CAP_EXP, 2))(routes_keys, routes_turns).reshape((DEVICES * SEQ, TOP))
    route_scale = jnp.clip(jnp.exp(math.log(1.0) - 2.3025851 * jax.random.uniform(seeds[4], (DEVICES * SEQ, TOP), jnp.float32) ** steps_of(seeds[4], (DEVICES * SEQ, TOP), ((0, 1024),), -0.2, 0.2)), 0.1, 1.0)
    w_gate = scatter_about(seeds[5], (EXPERTS, D, H), D ** -0.5, 0.125, ((0, 64), (2, 2)))
    w_up = scatter_about(seeds[6], (EXPERTS, D, H), D ** -0.5, 0.125, ((0, 64), (2, 2)))
    w_down = scatter_about(seeds[7], (EXPERTS, H, D), H ** -0.5, 0.21875, ((0, 64), (1, 2)))
    return {"image_rows": image_rows, "image_counts": image_counts, "image_owner": image_owner, "routes": routes, "route_scale": route_scale, "w_gate": w_gate, "w_up": w_up, "w_down": w_down}


def build_sequences(image_rows, image_counts, image_owner):
    owners = N_DP * N_MP
    slot_rows = SEQ // owners
    stacked = image_rows.reshape(DEVICES, IMG_ROWS, D)
    owner_ids = jnp.arange(owners, dtype=jnp.int32)
    placed_at = image_owner[:, None, :] == owner_ids[None, :, None]
    starts = (jnp.cumsum(image_counts, axis=1) - image_counts).astype(jnp.int32)
    count_to = jnp.sum(jnp.where(placed_at, image_counts[:, None, :], 0), axis=2).astype(jnp.int32)
    start_to = jnp.sum(jnp.where(placed_at, starts[:, None, :], 0), axis=2).astype(jnp.int32)
    within = jnp.arange(slot_rows, dtype=jnp.int32)
    row_index = jnp.clip(start_to[:, :, None] + within[None, None, :], 0, IMG_ROWS - 1).astype(jnp.int32)
    inside = within[None, None, :] < count_to[:, :, None]
    picked = jax.vmap(lambda source, where_rows: source[where_rows])(stacked, row_index.reshape(DEVICES, owners * slot_rows))
    picked = picked.reshape(DEVICES, owners, slot_rows, D)
    outgoing = jnp.where(inside[..., None], picked, jnp.zeros((), picked.dtype))
    grid = outgoing.reshape(N_DP, N_EXPERT, N_MP, N_DP, N_MP, slot_rows, D)
    grid = jnp.transpose(grid, (3, 1, 4, 0, 2, 5, 6))
    return grid.reshape(DEVICES * SEQ, D)


def reference(image_rows, image_counts, image_owner, routes, route_scale, w_gate, w_up, w_down):
    sequence = build_sequences(image_rows, image_counts, image_owner)
    share = route_scale / jnp.sum(route_scale, axis=1, keepdims=True)
    bound = DEVICES * CAP_EXP
    half_width = H // N_MP

    def one_expert(total, expert_id):
        hits = routes == expert_id
        chosen = jnp.any(hits, axis=1)
        weight_of = jnp.sum(jnp.where(hits, share, 0.0), axis=1)
        rows_at = jnp.nonzero(chosen, size=bound, fill_value=0)[0].astype(jnp.int32)
        live = jnp.arange(bound, dtype=jnp.int32) < jnp.sum(chosen.astype(jnp.int32))
        rows = sequence[rows_at]
        gate_sum = jnp.dot(rows, w_gate[expert_id], preferred_element_type=jnp.float32)
        up_sum = jnp.dot(rows, w_up[expert_id], preferred_element_type=jnp.float32)
        activated = (jax.nn.silu(gate_sum) * up_sum).astype(jnp.bfloat16)
        down_rows = w_down[expert_id]
        result = jnp.zeros((bound, D), jnp.float32)
        for core in range(N_MP):
            partial_out = jnp.dot(activated[:, core * half_width:(core + 1) * half_width], down_rows[core * half_width:(core + 1) * half_width], preferred_element_type=jnp.float32).astype(jnp.bfloat16)
            result = result + lax.optimization_barrier(partial_out).astype(jnp.float32)
        expert_out = result.astype(jnp.bfloat16)
        scaled = jnp.where(live[:, None], weight_of[rows_at][:, None] * expert_out.astype(jnp.float32), 0.0)
        return total.at[rows_at].add(scaled), None

    combined, unused = lax.scan(one_expert, jnp.zeros((DEVICES * SEQ, D), jnp.float32), jnp.arange(EXPERTS, dtype=jnp.int32))
    return combined.astype(jnp.bfloat16)
```

```python
import jax
import jax.numpy as jnp
from jax import lax
from jax.experimental import pallas as pl
from jax.experimental.pallas import tpu as pltpu
from jax.sharding import PartitionSpec as P

BF16 = jnp.bfloat16
F32 = jnp.float32
I32 = jnp.int32
VMEM = pl.BlockSpec(memory_space=pltpu.VMEM)

CAP = 6
GROUP = 8
BLOCKS = 3


def iota(shape, dim):
    return lax.broadcasted_iota(I32, shape, dim)


def dot(a, b):
    return jnp.dot(a, b, preferred_element_type=F32)


def pack_kernel(counts_ref, owner_ref, rows_ref, out_ref):
    images = counts_ref.shape[1]
    length, slot = out_ref.shape[0], out_ref.shape[0] // images
    counts = counts_ref[...]
    row = iota((length, images), 0)
    image = iota((length, images), 1)
    placed = owner_ref[...] == row // slot
    count = jnp.sum(jnp.where(placed, counts, 0), axis=1, keepdims=True)
    index = jnp.sum(jnp.where(placed, image, 0), axis=1, keepdims=True)
    start = jnp.sum(jnp.where(image < index, counts, 0), axis=1, keepdims=True)
    within = iota((length, 1), 0) % slot
    source = jnp.where(within < count, start + within, -1)
    pick = (iota((length, rows_ref.shape[0]), 1) == source).astype(F32).astype(BF16)
    out_ref[...] = dot(pick, rows_ref[...]).astype(BF16)


def dispatch_kernel(routes_ref, rows_ref, out_ref):
    length, width = rows_ref.shape
    experts = out_ref.shape[0] // GROUP
    block = width // (BLOCKS + 1)
    expert = iota((experts, length), 0)
    named = (expert == routes_ref[0:1, :]) | (expert == routes_ref[1:2, :])
    earlier = (iota((length, length), 0) < iota((length, length), 1)).astype(F32).astype(BF16)
    position = dot(named.astype(F32).astype(BF16), earlier)
    position = jnp.where(named, position, -1.0)[:, None, :]
    k = iota((experts, GROUP, length), 1)

    def placed(wanted):
        hit = position == wanted.astype(F32)
        return hit.astype(F32).reshape(experts * GROUP, length).astype(BF16)

    main = placed(jnp.where(k < CAP, k, -2))
    tail_rows = rows_ref[:, BLOCKS * block :]
    for j in range(BLOCKS):
        tail = placed(jnp.where(k == CAP, j, jnp.where(k == CAP + 1, BLOCKS + j, -2)))
        both = jnp.concatenate([main, tail], axis=1)
        source = jnp.concatenate([rows_ref[:, j * block : (j + 1) * block], tail_rows], axis=0)
        out_ref[:, j * block : (j + 1) * block] = dot(both, source).astype(BF16)


def expert_kernel(x_ref, gate_a, up_a, down_a, gate_b, up_b, down_b, out_ref, tail_ref, act_ref):
    rows, wide = x_ref.shape
    block = wide // BLOCKS
    half = gate_a.shape[1]
    step = 128
    r = iota((step, step), 0)
    c = iota((step, step), 1)
    same = r // GROUP == c // GROUP
    k_r, k_c = r % GROUP, c % GROUP

    def onehot(mask):
        return (same & mask).astype(F32).astype(BF16)

    gather = jnp.concatenate(
        [
            onehot(((k_r == j) & (k_c == CAP)) | ((k_r == BLOCKS + j) & (k_c == CAP + 1)))
            for j in range(BLOCKS)
        ],
        axis=1,
    )
    for g in range(rows // step):
        at = slice(g * step, (g + 1) * step)
        stacked = jnp.concatenate(
            [x_ref[at, j * block : (j + 1) * block] for j in range(BLOCKS)], axis=0
        )
        tail_ref[at, :] = dot(gather, stacked).astype(BF16)

    for at, gate_ref, up_ref in ((0, gate_a, up_a), (half, gate_b, up_b)):
        gate = dot(x_ref[...], gate_ref[:wide, :]) + dot(tail_ref[...], gate_ref[wide:, :])
        up = dot(x_ref[...], up_ref[:wide, :]) + dot(tail_ref[...], up_ref[wide:, :])
        act_ref[:, at : at + half] = (gate / (1.0 + jnp.exp(-gate)) * up).astype(BF16)

    def down(at):
        return dot(act_ref[:, :half], down_a[:, at : at + block]) + dot(
            act_ref[:, half:], down_b[:, at : at + block]
        )

    tail_ref[...] = down(wide).astype(BF16)
    is_slot = iota((step, block), 0) % GROUP < CAP
    for j in range(BLOCKS):
        spread = onehot(((k_c == j) & (k_r == CAP)) | ((k_c == BLOCKS + j) & (k_r == CAP + 1)))
        main = down(j * block)
        for g in range(rows // step):
            at = slice(g * step, (g + 1) * step)
            moved = dot(spread, tail_ref[at, :])
            out_ref[at, j * block : (j + 1) * block] = jnp.where(is_slot, main[at, :], moved).astype(
                BF16
            )


def combine_kernel(routes_ref, scale_ref, back_ref, out_ref):
    length = routes_ref.shape[0]
    slots = back_ref.shape[0]
    experts = slots // GROUP
    block = back_ref.shape[1] // BLOCKS
    scale = scale_ref[...]
    share = scale / jnp.sum(scale, axis=1, keepdims=True)
    expert = iota((length, experts), 1)
    hits = [expert == routes_ref[:, r : r + 1] for r in range(2)]
    named = (hits[0] | hits[1]).astype(F32).astype(BF16)
    earlier = (iota((length, length), 1) < iota((length, length), 0)).astype(F32).astype(BF16)
    position = dot(earlier, named)
    slot = iota((length, slots), 1)
    at = []
    for r in range(2):
        k = jnp.sum(jnp.where(hits[r], position, 0.0), axis=1, keepdims=True).astype(I32)
        at.append((k, routes_ref[:, r : r + 1] * GROUP))

    def onehot(index):
        return (slot == index).astype(F32).astype(BF16)

    main = [onehot(base + k) for k, base in at]
    tails = [jnp.zeros((length, block), F32) for _ in range(2)]
    for j in range(BLOCKS):
        picks = list(main)
        for k, base in at:
            second = k >= BLOCKS
            mine = jnp.where(second, k - BLOCKS, k) == j
            picks.append(onehot(jnp.where(mine, base + CAP + second.astype(I32), -1)))
        got = dot(jnp.concatenate(picks, axis=0), back_ref[:, j * block : (j + 1) * block])
        total = share[:, 0:1] * got[:length] + share[:, 1:2] * got[length : 2 * length]
        out_ref[:, j * block : (j + 1) * block] = total.astype(BF16)
        for r in range(2):
            tails[r] = tails[r] + got[(2 + r) * length : (3 + r) * length]
    total = share[:, 0:1] * tails[0] + share[:, 1:2] * tails[1]
    out_ref[:, BLOCKS * block :] = total.astype(BF16)


def call(kernel, out, *args, flops, scratch=(), limit=32 << 20):
    moved = sum(a.size * a.dtype.itemsize for a in args) + out[0] * out[1] * 2
    return pl.pallas_call(
        kernel,
        out_shape=jax.ShapeDtypeStruct(out, BF16),
        in_specs=[VMEM] * len(args),
        out_specs=VMEM,
        scratch_shapes=list(scratch),
        compiler_params=pltpu.CompilerParams(vmem_limit_bytes=limit),
        cost_estimate=pl.CostEstimate(flops=flops, bytes_accessed=moved, transcendentals=0),
    )(*args)


def local(image_rows, image_counts, image_owner, routes, route_scale, w_gate, w_up, w_down):
    owners = lax.axis_size(("dp", "mp"))
    experts = lax.axis_size("expert")
    length = routes.shape[0]
    width = image_rows.shape[1]
    slots = experts * GROUP
    wide = width // (BLOCKS + 1) * BLOCKS
    own = [w_gate[0], w_up[0], w_down[0]]
    half = own[0].shape[1]
    other = [lax.ppermute(w, "mp", [(0, 1), (1, 0)]) for w in own]

    outgoing = call(
        pack_kernel,
        (length, width),
        image_counts,
        image_owner,
        image_rows,
        flops=2 * length * image_rows.shape[0] * width,
    )
    arrived = lax.all_to_all(
        outgoing.reshape(owners, length // owners, width),
        ("dp", "mp"),
        split_axis=0,
        concat_axis=0,
        tiled=True,
    )
    sequence = arrived.reshape(length, width)
    buffer = call(
        dispatch_kernel, (slots, wide), routes.T, sequence, flops=4 * slots * length * wide
    )

    def exchange(x):
        y = lax.all_to_all(
            x.reshape(experts, GROUP, wide), "expert", split_axis=0, concat_axis=0, tiled=True
        )
        return y.reshape(slots, wide)

    received = exchange(buffer)
    result = call(
        expert_kernel,
        (slots, wide),
        received,
        *own,
        *other,
        flops=12 * slots * width * half,
        scratch=[pltpu.VMEM((slots, wide // BLOCKS), BF16), pltpu.VMEM((slots, 2 * half), BF16)],
    )
    returned = exchange(result)
    return call(
        combine_kernel,
        (length, width),
        routes,
        route_scale,
        returned,
        flops=8 * length * slots * wide,
    )


def solution(mesh):
    return jax.shard_map(
        local,
        mesh=mesh,
        in_specs=(
            P(("dp", "expert", "mp"), None),
            P(("dp", "expert", "mp"), None),
            P(("dp", "expert", "mp"), None),
            P(("dp", "expert", "mp"), None),
            P(("dp", "expert", "mp"), None),
            P("expert", None, "mp"),
            P("expert", None, "mp"),
            P("expert", "mp", None),
        ),
        out_specs=P(("dp", "expert", "mp"), None),
        check_vma=False,
    )
```

```python
import jax
import jax.numpy as jnp
from jax import lax
from jax.experimental import pallas as pl
from jax.experimental.pallas import tpu as pltpu
from jax.sharding import PartitionSpec as P

BF16 = jnp.bfloat16
F32 = jnp.float32
I32 = jnp.int32
VMEM = pl.BlockSpec(memory_space=pltpu.VMEM)
ANY = pl.BlockSpec(memory_space=pl.ANY)

CAP = 6
GROUP = 8
BLOCKS = 3


def iota(shape, dim):
    return lax.broadcasted_iota(I32, shape, dim)


def dot(a, b):
    return jnp.dot(a, b, preferred_element_type=F32)


def start(*pairs):
    copies = [pltpu.make_async_copy(*pair) for pair in pairs]
    for copy in copies:
        copy.start()
    return copies


def finish(copies):
    for copy in copies:
        copy.wait()


def pack_kernel(
    counts_hbm, owner_hbm, rows_hbm, out_hbm, counts_ref, owner_ref, rows_ref, out_ref, sems
):
    small = start(
        (counts_hbm, counts_ref, sems.at[0]),
        (owner_hbm, owner_ref, sems.at[1]),
    )
    large = start((rows_hbm, rows_ref, sems.at[2]))
    finish(small)
    images = counts_ref.shape[1]
    length, slot = out_ref.shape[0], out_ref.shape[0] // images
    counts = counts_ref[...]
    row = iota((length, images), 0)
    image = iota((length, images), 1)
    placed = owner_ref[...] == row // slot
    count = jnp.sum(jnp.where(placed, counts, 0), axis=1, keepdims=True)
    index = jnp.sum(jnp.where(placed, image, 0), axis=1, keepdims=True)
    first = jnp.sum(jnp.where(image < index, counts, 0), axis=1, keepdims=True)
    within = iota((length, 1), 0) % slot
    source = jnp.where(within < count, first + within, -1)
    pick = (iota((length, rows_ref.shape[0]), 1) == source).astype(F32).astype(BF16)
    finish(large)
    out_ref[...] = dot(pick, rows_ref[...]).astype(BF16)
    finish(start((out_ref, out_hbm, sems.at[3])))


def dispatch_kernel(routes_ref, rows_ref, out_hbm, out_ref, sems):
    length, width = rows_ref.shape
    experts = out_ref.shape[0] // GROUP
    block = width // (BLOCKS + 1)
    expert = iota((experts, length), 0)
    named = (expert == routes_ref[0:1, :]) | (expert == routes_ref[1:2, :])
    earlier = (iota((length, length), 0) < iota((length, length), 1)).astype(F32).astype(BF16)
    position = dot(named.astype(F32).astype(BF16), earlier)
    position = jnp.where(named, position, -1.0)[:, None, :]
    k = iota((experts, GROUP, length), 1)

    def placed(wanted):
        hit = position == wanted.astype(F32)
        return hit.astype(F32).reshape(experts * GROUP, length).astype(BF16)

    main = placed(jnp.where(k < CAP, k, -2))
    tail_rows = rows_ref[:, BLOCKS * block :]
    copies = []
    for j in range(BLOCKS):
        at = slice(j * block, (j + 1) * block)
        tail = placed(jnp.where(k == CAP, j, jnp.where(k == CAP + 1, BLOCKS + j, -2)))
        both = jnp.concatenate([main, tail], axis=1)
        source = jnp.concatenate([rows_ref[:, at], tail_rows], axis=0)
        out_ref[:, at] = dot(both, source).astype(BF16)
        copies += start((out_ref.at[:, at], out_hbm.at[:, at], sems.at[j]))
    finish(copies)


def expert_kernel(
    x_ref, gate_a, up_a, down_a, gate_b, up_b, down_b, out_hbm,
    gate_ref, up_ref, down_ref, rows_ref, act_ref, out_ref, sems,
):
    chunk_rows, wide = x_ref.shape
    block = wide // BLOCKS
    half = gate_a.shape[1]
    low, high = slice(0, half), slice(half, 2 * half)
    first, second = slice(0, gate_a.shape[0] // 2), slice(gate_a.shape[0] // 2, gate_a.shape[0])
    parts = [
        start(
            (gate_a.at[k], gate_ref.at[k, low], sems.at[4 * i]),
            (gate_b.at[k], gate_ref.at[k, high], sems.at[4 * i + 1]),
            (up_a.at[k], up_ref.at[k, low], sems.at[4 * i + 2]),
            (up_b.at[k], up_ref.at[k, high], sems.at[4 * i + 3]),
        )
        for i, k in enumerate((first, second))
    ]
    downs = start((down_a, down_ref.at[low], sems.at[8]), (down_b, down_ref.at[high], sems.at[9]))

    step = 256
    chunks = step // GROUP
    packed = chunks * CAP

    def onehot(q, c, j=None):
        k, sub = q // chunks, c % GROUP
        if j is None:
            hit = sub == k
        else:
            hit = ((k == j) & (sub == CAP)) | ((k == BLOCKS + j) & (sub == CAP + 1))
        hit = hit & (c // GROUP == q % chunks)
        return hit.astype(F32).astype(BF16)

    q, c = iota((packed, step), 0), iota((packed, step), 1)
    main = onehot(q, c)
    tail = jnp.concatenate([onehot(q, c, j) for j in range(BLOCKS)], axis=1)
    groups = range(chunk_rows // step)
    for g in groups:
        source, target = slice(g * step, (g + 1) * step), slice(g * packed, (g + 1) * packed)
        rows_ref[target, :wide] = dot(main, x_ref[source, :]).astype(BF16)
        stacked = jnp.concatenate(
            [x_ref[source, j * block : (j + 1) * block] for j in range(BLOCKS)], axis=0
        )
        rows_ref[target, wide:] = dot(tail, stacked).astype(BF16)

    finish(parts[0])
    gate, up = dot(rows_ref[:, first], gate_ref[first]), dot(rows_ref[:, first], up_ref[first])
    finish(parts[1])
    gate = gate + dot(rows_ref[:, second], gate_ref[second])
    up = up + dot(rows_ref[:, second], up_ref[second])
    act_ref[...] = (gate / (1.0 + jnp.exp(-gate)) * up).astype(BF16)
    finish(downs)
    last = dot(act_ref[...], down_ref[:, wide:]).astype(BF16)
    q, c = iota((step, packed), 1), iota((step, packed), 0)
    main = onehot(q, c)
    copies = []
    for j in range(BLOCKS):
        at = slice(j * block, (j + 1) * block)
        spread = jnp.concatenate([main, onehot(q, c, j)], axis=1)
        result = dot(act_ref[...], down_ref[:, at]).astype(BF16)
        for g in groups:
            source, target = slice(g * packed, (g + 1) * packed), slice(g * step, (g + 1) * step)
            both = jnp.concatenate([result[source], last[source]], axis=0)
            out_ref[target, at] = dot(spread, both).astype(BF16)
        copies += start((out_ref.at[:, at], out_hbm.at[:, at], sems.at[10 + j]))
    finish(copies)


def combine_kernel(routes_ref, scale_ref, back_ref, out_hbm, out_ref, sems):
    length = routes_ref.shape[0]
    slots = back_ref.shape[0]
    experts = slots // GROUP
    block = back_ref.shape[1] // BLOCKS
    scale = scale_ref[...]
    share = scale / jnp.sum(scale, axis=1, keepdims=True)
    expert = iota((length, experts), 1)
    hits = [expert == routes_ref[:, r : r + 1] for r in range(2)]
    named = (hits[0] | hits[1]).astype(F32).astype(BF16)
    earlier = (iota((length, length), 1) < iota((length, length), 0)).astype(F32).astype(BF16)
    position = dot(earlier, named)
    slot = iota((length, slots), 1)
    places = []
    for r in range(2):
        k = jnp.sum(jnp.where(hits[r], position, 0.0), axis=1, keepdims=True).astype(I32)
        places.append((k, routes_ref[:, r : r + 1] * GROUP))

    def onehot(index):
        return (slot == index).astype(F32).astype(BF16)

    main = [onehot(base + k) for k, base in places]
    tails = [jnp.zeros((length, block), F32) for _ in range(2)]
    copies = []
    for j in range(BLOCKS):
        at = slice(j * block, (j + 1) * block)
        picks = list(main)
        for k, base in places:
            second = k >= BLOCKS
            mine = jnp.where(second, k - BLOCKS, k) == j
            picks.append(onehot(jnp.where(mine, base + CAP + second.astype(I32), -1)))
        got = dot(jnp.concatenate(picks, axis=0), back_ref[:, at])
        total = share[:, 0:1] * got[:length] + share[:, 1:2] * got[length : 2 * length]
        out_ref[:, at] = total.astype(BF16)
        copies += start((out_ref.at[:, at], out_hbm.at[:, at], sems.at[j]))
        for r in range(2):
            tails[r] = tails[r] + got[(2 + r) * length : (3 + r) * length]
    total = share[:, 0:1] * tails[0] + share[:, 1:2] * tails[1]
    at = slice(BLOCKS * block, (BLOCKS + 1) * block)
    out_ref[:, at] = total.astype(BF16)
    finish(copies + start((out_ref.at[:, at], out_hbm.at[:, at], sems.at[BLOCKS])))


def call(kernel, out, *args, flops, scratch, sems, here=(), limit=32 << 20):
    moved = sum(a.size * a.dtype.itemsize for a in args) + out[0] * out[1] * 2
    return pl.pallas_call(
        kernel,
        out_shape=jax.ShapeDtypeStruct(out, BF16),
        in_specs=[VMEM if i in here else ANY for i in range(len(args))],
        out_specs=ANY,
        scratch_shapes=[pltpu.VMEM(*s) for s in scratch] + [pltpu.SemaphoreType.DMA((sems,))],
        compiler_params=pltpu.CompilerParams(vmem_limit_bytes=limit),
        cost_estimate=pl.CostEstimate(flops=flops, bytes_accessed=moved, transcendentals=0),
    )(*args)


def pack(counts, owner, rows, length):
    width = rows.shape[1]
    return call(
        pack_kernel, (length, width), counts, owner, rows,
        flops=2 * length * rows.shape[0] * width,
        scratch=[
            (counts.shape, I32), (owner.shape, I32), (rows.shape, BF16), ((length, width), BF16),
        ],
        sems=4, limit=62 << 20,
    )


def dispatch(routes_t, sequence, slots, wide):
    length = sequence.shape[0]
    return call(
        dispatch_kernel, (slots, wide), routes_t, sequence,
        flops=4 * slots * length * wide,
        scratch=[((slots, wide), BF16)], sems=BLOCKS, here=(0, 1),
    )


def run_expert(received, own, other):
    slots, wide = received.shape
    width, half = own[0].shape
    rows = slots // GROUP * CAP
    return call(
        expert_kernel, (slots, wide), received, *own, *other,
        flops=12 * slots * width * half,
        scratch=[
            ((width, 2 * half), BF16), ((width, 2 * half), BF16), ((2 * half, width), BF16),
            ((rows, width), BF16), ((rows, 2 * half), BF16), ((slots, wide), BF16),
        ],
        sems=10 + BLOCKS, here=(0,), limit=48 << 20,
    )


def combine(routes, route_scale, returned, width):
    length, slots = routes.shape[0], returned.shape[0]
    return call(
        combine_kernel, (length, width), routes, route_scale, returned,
        flops=8 * length * slots * returned.shape[1],
        scratch=[((length, width), BF16)], sems=BLOCKS + 1, here=(0, 1, 2),
    )


def local(image_rows, image_counts, image_owner, routes, route_scale, w_gate, w_up, w_down):
    owners = lax.axis_size(("dp", "mp"))
    experts = lax.axis_size("expert")
    length = routes.shape[0]
    width = image_rows.shape[1]
    slots = experts * GROUP
    wide = width // (BLOCKS + 1) * BLOCKS
    own = [w_gate[0], w_up[0], w_down[0]]
    other = [lax.ppermute(w, "mp", [(0, 1), (1, 0)]) for w in own]

    outgoing = pack(image_counts, image_owner, image_rows, length)
    arrived = lax.all_to_all(
        outgoing.reshape(owners, length // owners, width),
        ("dp", "mp"),
        split_axis=0,
        concat_axis=0,
        tiled=True,
    )
    buffer = dispatch(routes.T, arrived.reshape(length, width), slots, wide)

    def exchange(x):
        y = lax.all_to_all(
            x.reshape(experts, GROUP, wide), "expert", split_axis=0, concat_axis=0, tiled=True
        )
        return y.reshape(slots, wide)

    returned = exchange(run_expert(exchange(buffer), own, other))
    return combine(routes, route_scale, returned, width)


def solution(mesh):
    return jax.shard_map(
        local,
        mesh=mesh,
        in_specs=(
            P(("dp", "expert", "mp"), None),
            P(("dp", "expert", "mp"), None),
            P(("dp", "expert", "mp"), None),
            P(("dp", "expert", "mp"), None),
            P(("dp", "expert", "mp"), None),
            P("expert", None, "mp"),
            P("expert", None, "mp"),
            P("expert", "mp", None),
        ),
        out_specs=P(("dp", "expert", "mp"), None),
        check_vma=False,
    )
```

```python
import jax
import jax.numpy as jnp
from jax import lax
from jax.experimental import pallas as pl
from jax.experimental.pallas import tpu as pltpu
from jax.sharding import PartitionSpec as P

BF16 = jnp.bfloat16
F32 = jnp.float32
I32 = jnp.int32
VMEM = pl.BlockSpec(memory_space=pltpu.VMEM)
ANY = pl.BlockSpec(memory_space=pl.ANY)

CAP = 6
GROUP = 8
BLOCKS = 3


def iota(shape, dim):
    return lax.broadcasted_iota(I32, shape, dim)


def dot(a, b):
    return jnp.dot(a, b, preferred_element_type=F32)


def start(*pairs):
    copies = [pltpu.make_async_copy(*pair) for pair in pairs]
    for copy in copies:
        copy.start()
    return copies


def finish(copies):
    for copy in copies:
        copy.wait()


def pack_kernel(
    counts_hbm, owner_hbm, rows_hbm, out_hbm, counts_ref, owner_ref, rows_ref, out_ref, sems
):
    small = start(
        (counts_hbm, counts_ref, sems.at[0]),
        (owner_hbm, owner_ref, sems.at[1]),
    )
    large = start((rows_hbm, rows_ref, sems.at[2]))
    finish(small)
    images = counts_ref.shape[1]
    length, slot = out_ref.shape[0], out_ref.shape[0] // images
    counts = counts_ref[...]
    row = iota((length, images), 0)
    image = iota((length, images), 1)
    placed = owner_ref[...] == row // slot
    count = jnp.sum(jnp.where(placed, counts, 0), axis=1, keepdims=True)
    index = jnp.sum(jnp.where(placed, image, 0), axis=1, keepdims=True)
    first = jnp.sum(jnp.where(image < index, counts, 0), axis=1, keepdims=True)
    within = iota((length, 1), 0) % slot
    source = jnp.where(within < count, first + within, -1)
    pick = (iota((length, rows_ref.shape[0]), 1) == source).astype(F32).astype(BF16)
    finish(large)
    out_ref[...] = dot(pick, rows_ref[...]).astype(BF16)
    finish(start((out_ref, out_hbm, sems.at[3])))


def dispatch_kernel(routes_ref, rows_ref, out_hbm, out_ref, sems):
    length, width = rows_ref.shape
    experts = out_ref.shape[0] // GROUP
    block = width // (BLOCKS + 1)
    expert = iota((experts, length), 0)
    named = (expert == routes_ref[0:1, :]) | (expert == routes_ref[1:2, :])
    earlier = (iota((length, length), 0) < iota((length, length), 1)).astype(F32).astype(BF16)
    position = dot(named.astype(F32).astype(BF16), earlier)
    position = jnp.where(named, position, -1.0)[:, None, :]
    k = iota((experts, GROUP, length), 1)

    def placed(wanted):
        hit = position == wanted.astype(F32)
        return hit.astype(F32).reshape(experts * GROUP, length).astype(BF16)

    main = placed(jnp.where(k < CAP, k, -2))
    tail_rows = rows_ref[:, BLOCKS * block :]
    copies = []
    for j in range(BLOCKS):
        at = slice(j * block, (j + 1) * block)
        tail = placed(jnp.where(k == CAP, j, jnp.where(k == CAP + 1, BLOCKS + j, -2)))
        both = jnp.concatenate([main, tail], axis=1)
        source = jnp.concatenate([rows_ref[:, at], tail_rows], axis=0)
        out_ref[:, at] = dot(both, source).astype(BF16)
        copies += start((out_ref.at[:, at], out_hbm.at[:, at], sems.at[j]))
    finish(copies)


def expert_kernel(
    x_ref, gate_a, up_a, down_a, gate_b, up_b, down_b, out_hbm,
    gate_ref, up_ref, down_ref, rows_ref, act_ref, out_ref, sems,
):
    chunk_rows, wide = x_ref.shape
    block = wide // BLOCKS
    half = gate_a.shape[1]
    low, high = slice(0, half), slice(half, 2 * half)
    cuts = 4
    deep = gate_a.shape[0] // cuts
    steps = [slice(i * deep, (i + 1) * deep) for i in range(cuts)]
    parts = [
        start(
            (gate_a.at[k], gate_ref.at[k, low], sems.at[4 * i]),
            (gate_b.at[k], gate_ref.at[k, high], sems.at[4 * i + 1]),
            (up_a.at[k], up_ref.at[k, low], sems.at[4 * i + 2]),
            (up_b.at[k], up_ref.at[k, high], sems.at[4 * i + 3]),
        )
        for i, k in enumerate(steps)
    ]
    downs = start(
        (down_a, down_ref.at[low], sems.at[4 * cuts]),
        (down_b, down_ref.at[high], sems.at[4 * cuts + 1]),
    )

    step = 256
    chunks = step // GROUP
    packed = chunks * CAP

    def onehot(t, c):
        return ((c // GROUP == t % chunks) & (c % GROUP == t // chunks)).astype(F32).astype(BF16)

    gather = onehot(iota((step, step), 0), iota((step, step), 1))
    spread = onehot(iota((step, step), 1), iota((step, step), 0))
    groups = range(chunk_rows // step)
    for g in groups:
        for j in range(BLOCKS):
            at = slice(j * block, (j + 1) * block)
            moved = dot(gather, x_ref[g * step : (g + 1) * step, at]).astype(BF16)
            rows_ref[g * packed : (g + 1) * packed, at] = moved[:packed]
            for i, k in enumerate((j, BLOCKS + j)):
                target = g * packed + k * chunks
                rows_ref[target : target + chunks, wide:] = moved[packed + i * chunks :][:chunks]

    gate = up = 0.0
    for k, copies in zip(steps, parts):
        finish(copies)
        gate = gate + dot(rows_ref[:, k], gate_ref[k])
        up = up + dot(rows_ref[:, k], up_ref[k])
    act_ref[...] = (gate / (1.0 + jnp.exp(-gate)) * up).astype(BF16)
    finish(downs)
    last = dot(act_ref[...], down_ref[:, wide:]).astype(BF16)
    copies = []
    for j in range(BLOCKS):
        at = slice(j * block, (j + 1) * block)
        result = dot(act_ref[...], down_ref[:, at]).astype(BF16)
        for g in groups:
            source, target = g * packed, slice(g * step, (g + 1) * step)
            tails = [source + (j + k) * chunks for k in (0, BLOCKS)]
            both = [result[source : source + packed]] + [last[i : i + chunks] for i in tails]
            out_ref[target, at] = dot(spread, jnp.concatenate(both, axis=0)).astype(BF16)
        copies += start((out_ref.at[:, at], out_hbm.at[:, at], sems.at[4 * cuts + 2 + j]))
    finish(copies)


def places_kernel(routes_ref, scale_ref, at_ref, share_ref):
    length = routes_ref.shape[0]
    scale = scale_ref[...]
    share_ref[...] = scale / jnp.sum(scale, axis=1, keepdims=True)
    expert = iota((length, 128), 1)
    hits = [expert == routes_ref[:, r : r + 1] for r in range(2)]
    named = (hits[0] | hits[1]).astype(F32).astype(BF16)
    earlier = (iota((length, length), 1) < iota((length, length), 0)).astype(F32).astype(BF16)
    position = dot(earlier, named)
    for r in range(2):
        k = jnp.sum(jnp.where(hits[r], position, 0.0), axis=1, keepdims=True).astype(I32)
        at_ref[:, r : r + 1] = routes_ref[:, r : r + 1] * GROUP + k


def combine_kernel(at_ref, share_ref, back_ref, out_hbm, out_ref, sems):
    length = at_ref.shape[0]
    slots = back_ref.shape[0]
    block = back_ref.shape[1] // BLOCKS
    share = share_ref[...]
    slot = iota((length, slots), 1)
    places = [at_ref[:, r : r + 1] for r in range(2)]

    def onehot(index):
        return (slot == index).astype(F32).astype(BF16)

    main = [onehot(place) for place in places]
    tails = [jnp.zeros((length, block), F32) for _ in range(2)]
    copies = []
    for j in range(BLOCKS):
        at = slice(j * block, (j + 1) * block)
        picks = list(main)
        for place in places:
            k, base = place % GROUP, place - place % GROUP
            second = k >= BLOCKS
            mine = jnp.where(second, k - BLOCKS, k) == j
            picks.append(onehot(jnp.where(mine, base + CAP + second.astype(I32), -1)))
        got = dot(jnp.concatenate(picks, axis=0), back_ref[:, at])
        total = share[:, 0:1] * got[:length] + share[:, 1:2] * got[length : 2 * length]
        out_ref[:, at] = total.astype(BF16)
        copies += start((out_ref.at[:, at], out_hbm.at[:, at], sems.at[j]))
        for r in range(2):
            tails[r] = tails[r] + got[(2 + r) * length : (3 + r) * length]
    total = share[:, 0:1] * tails[0] + share[:, 1:2] * tails[1]
    at = slice(BLOCKS * block, (BLOCKS + 1) * block)
    out_ref[:, at] = total.astype(BF16)
    finish(copies + start((out_ref.at[:, at], out_hbm.at[:, at], sems.at[BLOCKS])))


def call(kernel, out, *args, flops, scratch, sems, here=(), limit=32 << 20):
    moved = sum(a.size * a.dtype.itemsize for a in args) + out[0] * out[1] * 2
    return pl.pallas_call(
        kernel,
        out_shape=jax.ShapeDtypeStruct(out, BF16),
        in_specs=[VMEM if i in here else ANY for i in range(len(args))],
        out_specs=ANY,
        scratch_shapes=[pltpu.VMEM(*s) for s in scratch] + [pltpu.SemaphoreType.DMA((sems,))],
        compiler_params=pltpu.CompilerParams(vmem_limit_bytes=limit),
        cost_estimate=pl.CostEstimate(flops=flops, bytes_accessed=moved, transcendentals=0),
    )(*args)


def pack(counts, owner, rows, length):
    width = rows.shape[1]
    return call(
        pack_kernel, (length, width), counts, owner, rows,
        flops=2 * length * rows.shape[0] * width,
        scratch=[
            (counts.shape, I32), (owner.shape, I32), (rows.shape, BF16), ((length, width), BF16),
        ],
        sems=4, limit=62 << 20,
    )


def dispatch(routes_t, sequence, slots, wide):
    length = sequence.shape[0]
    return call(
        dispatch_kernel, (slots, wide), routes_t, sequence,
        flops=4 * slots * length * wide,
        scratch=[((slots, wide), BF16)], sems=BLOCKS, here=(0, 1),
    )


def run_expert(received, own, other):
    slots, wide = received.shape
    width, half = own[0].shape
    rows = slots // GROUP * CAP
    return call(
        expert_kernel, (slots, wide), received, *own, *other,
        flops=12 * slots * width * half,
        scratch=[
            ((width, 2 * half), BF16), ((width, 2 * half), BF16), ((2 * half, width), BF16),
            ((rows, width), BF16), ((rows, 2 * half), BF16), ((slots, wide), BF16),
        ],
        sems=18 + BLOCKS, here=(0,), limit=48 << 20,
    )


def combine(routes, route_scale, returned, width):
    length, slots = routes.shape[0], returned.shape[0]
    at, share = pl.pallas_call(
        places_kernel,
        out_shape=[
            jax.ShapeDtypeStruct(routes.shape, I32),
            jax.ShapeDtypeStruct(routes.shape, F32),
        ],
        compiler_params=pltpu.CompilerParams(vmem_limit_bytes=16 << 20),
    )(routes, route_scale)
    return call(
        combine_kernel, (length, width), at, share, returned,
        flops=8 * length * slots * returned.shape[1],
        scratch=[((length, width), BF16)], sems=BLOCKS + 1, here=(0, 1, 2),
    )


def local(image_rows, image_counts, image_owner, routes, route_scale, w_gate, w_up, w_down):
    owners = lax.axis_size(("dp", "mp"))
    experts = lax.axis_size("expert")
    length = routes.shape[0]
    width = image_rows.shape[1]
    slots = experts * GROUP
    wide = width // (BLOCKS + 1) * BLOCKS
    own = [w_gate[0], w_up[0], w_down[0]]
    other = [lax.ppermute(w, "mp", [(0, 1), (1, 0)]) for w in own]

    outgoing = pack(image_counts, image_owner, image_rows, length)
    arrived = lax.all_to_all(
        outgoing.reshape(owners, length // owners, width),
        ("dp", "mp"),
        split_axis=0,
        concat_axis=0,
        tiled=True,
    )
    buffer = dispatch(routes.T, arrived.reshape(length, width), slots, wide)

    def exchange(x):
        y = lax.all_to_all(
            x.reshape(experts, GROUP, wide), "expert", split_axis=0, concat_axis=0, tiled=True
        )
        return y.reshape(slots, wide)

    returned = exchange(run_expert(exchange(buffer), own, other))
    return combine(routes, route_scale, returned, width)


def solution(mesh):
    return jax.shard_map(
        local,
        mesh=mesh,
        in_specs=(
            P(("dp", "expert", "mp"), None),
            P(("dp", "expert", "mp"), None),
            P(("dp", "expert", "mp"), None),
            P(("dp", "expert", "mp"), None),
            P(("dp", "expert", "mp"), None),
            P("expert", None, "mp"),
            P("expert", None, "mp"),
            P("expert", "mp", None),
        ),
        out_specs=P(("dp", "expert", "mp"), None),
        check_vma=False,
    )
```

```python
import jax
import jax.numpy as jnp
from jax import lax
from jax.experimental import pallas as pl
from jax.experimental.pallas import tpu as pltpu
from jax.sharding import PartitionSpec as P

BF16 = jnp.bfloat16
F32 = jnp.float32
I32 = jnp.int32
VMEM = pl.BlockSpec(memory_space=pltpu.VMEM)
ANY = pl.BlockSpec(memory_space=pl.ANY)

CAP = 6
GROUP = 8
BLOCKS = 3


def iota(shape, dim):
    return lax.broadcasted_iota(I32, shape, dim)


def dot(a, b):
    return jnp.dot(a, b, preferred_element_type=F32)


def start(*pairs):
    copies = [pltpu.make_async_copy(*pair) for pair in pairs]
    for copy in copies:
        copy.start()
    return copies


def finish(copies):
    for copy in copies:
        copy.wait()


def pack_kernel(
    counts_hbm, owner_hbm, rows_hbm, out_hbm, counts_ref, owner_ref, rows_ref, out_ref, sems
):
    small = start(
        (counts_hbm, counts_ref, sems.at[0]),
        (owner_hbm, owner_ref, sems.at[1]),
    )
    large = start((rows_hbm, rows_ref, sems.at[2]))
    finish(small)
    images = counts_ref.shape[1]
    length, slot = out_ref.shape[0], out_ref.shape[0] // images
    counts = counts_ref[...]
    row = iota((length, images), 0)
    image = iota((length, images), 1)
    placed = owner_ref[...] == row // slot
    count = jnp.sum(jnp.where(placed, counts, 0), axis=1, keepdims=True)
    index = jnp.sum(jnp.where(placed, image, 0), axis=1, keepdims=True)
    first = jnp.sum(jnp.where(image < index, counts, 0), axis=1, keepdims=True)
    within = iota((length, 1), 0) % slot
    source = jnp.where(within < count, first + within, -1)
    pick = (iota((length, rows_ref.shape[0]), 1) == source).astype(F32).astype(BF16)
    finish(large)
    out_ref[...] = dot(pick, rows_ref[...]).astype(BF16)
    finish(start((out_ref, out_hbm, sems.at[3])))


def slots_kernel(routes_ref, picks_ref):
    length = routes_ref.shape[1]
    experts = picks_ref.shape[0] // GROUP
    expert = iota((experts, length), 0)
    named = (expert == routes_ref[0:1, :]) | (expert == routes_ref[1:2, :])
    earlier = (iota((length, length), 0) < iota((length, length), 1)).astype(F32).astype(BF16)
    position = dot(named.astype(F32).astype(BF16), earlier)
    position = jnp.where(named, position, -1.0)[:, None, :]
    k = iota((experts, GROUP, length), 1)

    def placed(wanted):
        hit = position == wanted.astype(F32)
        return hit.astype(F32).reshape(experts * GROUP, length).astype(BF16)

    picks_ref[:, :length] = placed(jnp.where(k < CAP, k, -2))
    for j in range(BLOCKS):
        tail = placed(jnp.where(k == CAP, j, jnp.where(k == CAP + 1, BLOCKS + j, -2)))
        picks_ref[:, (j + 1) * length : (j + 2) * length] = tail


def dispatch_kernel(picks_ref, rows_ref, out_hbm, out_ref, sems):
    length, width = rows_ref.shape
    block = width // (BLOCKS + 1)
    main = picks_ref[:, :length]
    tail_rows = rows_ref[:, BLOCKS * block :]
    copies = []
    for j in range(BLOCKS):
        at = slice(j * block, (j + 1) * block)
        tail = picks_ref[:, (j + 1) * length : (j + 2) * length]
        both = jnp.concatenate([main, tail], axis=1)
        source = jnp.concatenate([rows_ref[:, at], tail_rows], axis=0)
        out_ref[:, at] = dot(both, source).astype(BF16)
        copies += start((out_ref.at[:, at], out_hbm.at[:, at], sems.at[j]))
    finish(copies)


def expert_kernel(
    x_ref, gate_a, up_a, down_a, gate_b, up_b, down_b, out_hbm,
    gate_ref, up_ref, down_ref, rows_ref, act_ref, out_ref, sems,
):
    chunk_rows, wide = x_ref.shape
    block = wide // BLOCKS
    half = gate_a.shape[1]
    low, high = slice(0, half), slice(half, 2 * half)
    cuts = 4
    deep = gate_a.shape[0] // cuts
    steps = [slice(i * deep, (i + 1) * deep) for i in range(cuts)]
    parts = [
        start(
            (gate_a.at[k], gate_ref.at[k, low], sems.at[4 * i]),
            (gate_b.at[k], gate_ref.at[k, high], sems.at[4 * i + 1]),
            (up_a.at[k], up_ref.at[k, low], sems.at[4 * i + 2]),
            (up_b.at[k], up_ref.at[k, high], sems.at[4 * i + 3]),
        )
        for i, k in enumerate(steps)
    ]
    downs = start(
        (down_a, down_ref.at[low], sems.at[4 * cuts]),
        (down_b, down_ref.at[high], sems.at[4 * cuts + 1]),
    )

    step = 256
    chunks = step // GROUP
    packed = chunks * CAP

    def onehot(t, c):
        return ((c // GROUP == t % chunks) & (c % GROUP == t // chunks)).astype(F32).astype(BF16)

    gather = onehot(iota((step, step), 0), iota((step, step), 1))
    spread = onehot(iota((step, step), 1), iota((step, step), 0))
    groups = range(chunk_rows // step)
    for g in groups:
        for j in range(BLOCKS):
            at = slice(j * block, (j + 1) * block)
            moved = dot(gather, x_ref[g * step : (g + 1) * step, at]).astype(BF16)
            rows_ref[g * packed : (g + 1) * packed, at] = moved[:packed]
            for i, k in enumerate((j, BLOCKS + j)):
                target = g * packed + k * chunks
                rows_ref[target : target + chunks, wide:] = moved[packed + i * chunks :][:chunks]

    gate = up = 0.0
    for k, copies in zip(steps, parts):
        finish(copies)
        gate = gate + dot(rows_ref[:, k], gate_ref[k])
        up = up + dot(rows_ref[:, k], up_ref[k])
    act_ref[...] = (gate / (1.0 + jnp.exp(-gate)) * up).astype(BF16)
    finish(downs)
    last = dot(act_ref[...], down_ref[:, wide:]).astype(BF16)
    copies = []
    for j in range(BLOCKS):
        at = slice(j * block, (j + 1) * block)
        result = dot(act_ref[...], down_ref[:, at]).astype(BF16)
        for g in groups:
            source, target = g * packed, slice(g * step, (g + 1) * step)
            tails = [source + (j + k) * chunks for k in (0, BLOCKS)]
            both = [result[source : source + packed]] + [last[i : i + chunks] for i in tails]
            out_ref[target, at] = dot(spread, jnp.concatenate(both, axis=0)).astype(BF16)
        copies += start((out_ref.at[:, at], out_hbm.at[:, at], sems.at[4 * cuts + 2 + j]))
    finish(copies)


def places_kernel(routes_ref, scale_ref, at_ref, share_ref):
    length = routes_ref.shape[0]
    scale = scale_ref[...]
    share_ref[...] = scale / jnp.sum(scale, axis=1, keepdims=True)
    expert = iota((length, 128), 1)
    hits = [expert == routes_ref[:, r : r + 1] for r in range(2)]
    named = (hits[0] | hits[1]).astype(F32).astype(BF16)
    earlier = (iota((length, length), 1) < iota((length, length), 0)).astype(F32).astype(BF16)
    position = dot(earlier, named)
    for r in range(2):
        k = jnp.sum(jnp.where(hits[r], position, 0.0), axis=1, keepdims=True).astype(I32)
        at_ref[:, r : r + 1] = routes_ref[:, r : r + 1] * GROUP + k


def combine_kernel(at_ref, share_ref, back_ref, out_hbm, out_ref, sems):
    length = at_ref.shape[0]
    slots = back_ref.shape[0]
    block = back_ref.shape[1] // BLOCKS
    share = share_ref[...]
    slot = iota((length, slots), 1)
    places = [at_ref[:, r : r + 1] for r in range(2)]

    def onehot(index):
        return (slot == index).astype(F32).astype(BF16)

    main = [onehot(place) for place in places]
    tails = [jnp.zeros((length, block), F32) for _ in range(2)]
    copies = []
    for j in range(BLOCKS):
        at = slice(j * block, (j + 1) * block)
        picks = list(main)
        for place in places:
            k, base = place % GROUP, place - place % GROUP
            second = k >= BLOCKS
            mine = jnp.where(second, k - BLOCKS, k) == j
            picks.append(onehot(jnp.where(mine, base + CAP + second.astype(I32), -1)))
        got = dot(jnp.concatenate(picks, axis=0), back_ref[:, at])
        total = share[:, 0:1] * got[:length] + share[:, 1:2] * got[length : 2 * length]
        out_ref[:, at] = total.astype(BF16)
        copies += start((out_ref.at[:, at], out_hbm.at[:, at], sems.at[j]))
        for r in range(2):
            tails[r] = tails[r] + got[(2 + r) * length : (3 + r) * length]
    total = share[:, 0:1] * tails[0] + share[:, 1:2] * tails[1]
    at = slice(BLOCKS * block, (BLOCKS + 1) * block)
    out_ref[:, at] = total.astype(BF16)
    finish(copies + start((out_ref.at[:, at], out_hbm.at[:, at], sems.at[BLOCKS])))


def call(kernel, out, *args, flops, scratch, sems, here=(), limit=32 << 20):
    moved = sum(a.size * a.dtype.itemsize for a in args) + out[0] * out[1] * 2
    return pl.pallas_call(
        kernel,
        out_shape=jax.ShapeDtypeStruct(out, BF16),
        in_specs=[VMEM if i in here else ANY for i in range(len(args))],
        out_specs=ANY,
        scratch_shapes=[pltpu.VMEM(*s) for s in scratch] + [pltpu.SemaphoreType.DMA((sems,))],
        compiler_params=pltpu.CompilerParams(vmem_limit_bytes=limit),
        cost_estimate=pl.CostEstimate(flops=flops, bytes_accessed=moved, transcendentals=0),
    )(*args)


def pack(counts, owner, rows, length):
    width = rows.shape[1]
    return call(
        pack_kernel, (length, width), counts, owner, rows,
        flops=2 * length * rows.shape[0] * width,
        scratch=[
            (counts.shape, I32), (owner.shape, I32), (rows.shape, BF16), ((length, width), BF16),
        ],
        sems=4, limit=62 << 20,
    )


def find_slots(routes_t, slots):
    return pl.pallas_call(
        slots_kernel,
        out_shape=jax.ShapeDtypeStruct((slots, (BLOCKS + 1) * routes_t.shape[1]), BF16),
        compiler_params=pltpu.CompilerParams(vmem_limit_bytes=16 << 20),
    )(routes_t)


def dispatch(picks, sequence, wide):
    length, slots = sequence.shape[0], picks.shape[0]
    return call(
        dispatch_kernel, (slots, wide), picks, sequence,
        flops=4 * slots * length * wide,
        scratch=[((slots, wide), BF16)], sems=BLOCKS, here=(0, 1),
    )


def run_expert(received, own, other):
    slots, wide = received.shape
    width, half = own[0].shape
    rows = slots // GROUP * CAP
    return call(
        expert_kernel, (slots, wide), received, *own, *other,
        flops=12 * slots * width * half,
        scratch=[
            ((width, 2 * half), BF16), ((width, 2 * half), BF16), ((2 * half, width), BF16),
            ((rows, width), BF16), ((rows, 2 * half), BF16), ((slots, wide), BF16),
        ],
        sems=18 + BLOCKS, here=(0,), limit=48 << 20,
    )


def find_places(routes, route_scale):
    return pl.pallas_call(
        places_kernel,
        out_shape=[
            jax.ShapeDtypeStruct(routes.shape, I32),
            jax.ShapeDtypeStruct(routes.shape, F32),
        ],
        compiler_params=pltpu.CompilerParams(vmem_limit_bytes=16 << 20),
    )(routes, route_scale)


def combine(at, share, returned, width):
    length, slots = at.shape[0], returned.shape[0]
    return call(
        combine_kernel, (length, width), at, share, returned,
        flops=8 * length * slots * returned.shape[1],
        scratch=[((length, width), BF16)], sems=BLOCKS + 1, here=(0, 1, 2),
    )


def local(image_rows, image_counts, image_owner, routes, route_scale, w_gate, w_up, w_down):
    owners = lax.axis_size(("dp", "mp"))
    experts = lax.axis_size("expert")
    length = routes.shape[0]
    width = image_rows.shape[1]
    slots = experts * GROUP
    wide = width // (BLOCKS + 1) * BLOCKS
    own = [w_gate[0], w_up[0], w_down[0]]
    other = [lax.ppermute(w, "mp", [(0, 1), (1, 0)]) for w in own]

    outgoing = pack(image_counts, image_owner, image_rows, length)
    arrived = lax.all_to_all(
        outgoing.reshape(owners, length // owners, width),
        ("dp", "mp"),
        split_axis=0,
        concat_axis=0,
        tiled=True,
    )
    picks = find_slots(routes.T, slots)
    buffer = dispatch(picks, arrived.reshape(length, width), wide)

    def exchange(x):
        y = lax.all_to_all(
            x.reshape(experts, GROUP, wide), "expert", split_axis=0, concat_axis=0, tiled=True
        )
        return y.reshape(slots, wide)

    received = exchange(buffer)
    received, places = lax.optimization_barrier((received, find_places(routes, route_scale)))
    returned = exchange(run_expert(received, own, other))
    return combine(*places, returned, width)


def solution(mesh):
    return jax.shard_map(
        local,
        mesh=mesh,
        in_specs=(
            P(("dp", "expert", "mp"), None),
            P(("dp", "expert", "mp"), None),
            P(("dp", "expert", "mp"), None),
            P(("dp", "expert", "mp"), None),
            P(("dp", "expert", "mp"), None),
            P("expert", None, "mp"),
            P("expert", None, "mp"),
            P("expert", "mp", None),
        ),
        out_specs=P(("dp", "expert", "mp"), None),
        check_vma=False,
    )
```

```python
import jax
import jax.numpy as jnp
from jax import lax
from jax.experimental import pallas as pl
from jax.experimental.pallas import tpu as pltpu
from jax.sharding import PartitionSpec as P

BF16 = jnp.bfloat16
F32 = jnp.float32
I32 = jnp.int32
VMEM = pl.BlockSpec(memory_space=pltpu.VMEM)
ANY = pl.BlockSpec(memory_space=pl.ANY)

CAP = 6
GROUP = 8
BLOCKS = 3


def iota(shape, dim):
    return lax.broadcasted_iota(I32, shape, dim)


def dot(a, b):
    return jnp.dot(a, b, preferred_element_type=F32)


def start(*pairs):
    copies = [pltpu.make_async_copy(*pair) for pair in pairs]
    for copy in copies:
        copy.start()
    return copies


def finish(copies):
    for copy in copies:
        copy.wait()


def pack_kernel(
    counts_hbm, owner_hbm, rows_hbm, out_hbm, counts_ref, owner_ref, rows_ref, out_ref, sems
):
    small = start(
        (counts_hbm, counts_ref, sems.at[0]),
        (owner_hbm, owner_ref, sems.at[1]),
    )
    large = start((rows_hbm, rows_ref, sems.at[2]))
    finish(small)
    images = counts_ref.shape[1]
    length, slot = out_ref.shape[0], out_ref.shape[0] // images
    counts = counts_ref[...]
    row = iota((length, images), 0)
    image = iota((length, images), 1)
    placed = owner_ref[...] == row // slot
    count = jnp.sum(jnp.where(placed, counts, 0), axis=1, keepdims=True)
    index = jnp.sum(jnp.where(placed, image, 0), axis=1, keepdims=True)
    first = jnp.sum(jnp.where(image < index, counts, 0), axis=1, keepdims=True)
    within = iota((length, 1), 0) % slot
    source = jnp.where(within < count, first + within, -1)
    pick = (iota((length, rows_ref.shape[0]), 1) == source).astype(F32).astype(BF16)
    finish(large)
    out_ref[...] = dot(pick, rows_ref[...]).astype(BF16)
    finish(start((out_ref, out_hbm, sems.at[3])))


def slots_kernel(routes_ref, picks_ref):
    length = routes_ref.shape[1]
    experts = picks_ref.shape[0] // GROUP
    expert = iota((experts, length), 0)
    named = (expert == routes_ref[0:1, :]) | (expert == routes_ref[1:2, :])
    earlier = (iota((length, length), 0) < iota((length, length), 1)).astype(F32).astype(BF16)
    position = dot(named.astype(F32).astype(BF16), earlier)
    position = jnp.where(named, position, -1.0)[:, None, :]
    k = iota((experts, GROUP, length), 1)

    def placed(wanted):
        hit = position == wanted.astype(F32)
        return hit.astype(F32).reshape(experts * GROUP, length).astype(BF16)

    picks_ref[:, :length] = placed(jnp.where(k < CAP, k, -2))
    for j in range(BLOCKS):
        tail = placed(jnp.where(k == CAP, j, jnp.where(k == CAP + 1, BLOCKS + j, -2)))
        picks_ref[:, (j + 1) * length : (j + 2) * length] = tail


def dispatch_kernel(picks_ref, rows_ref, out_hbm, out_ref, sems):
    length, width = rows_ref.shape
    block = width // (BLOCKS + 1)
    main = picks_ref[:, :length]
    tail_rows = rows_ref[:, BLOCKS * block :]
    copies = []
    for j in range(BLOCKS):
        at = slice(j * block, (j + 1) * block)
        tail = picks_ref[:, (j + 1) * length : (j + 2) * length]
        both = jnp.concatenate([main, tail], axis=1)
        source = jnp.concatenate([rows_ref[:, at], tail_rows], axis=0)
        out_ref[:, at] = dot(both, source).astype(BF16)
        copies += start((out_ref.at[:, at], out_hbm.at[:, at], sems.at[j]))
    finish(copies)


def expert_kernel(
    x_ref, gate_a, up_a, down_a, gate_b, up_b, down_b, out_ref,
    gate_ref, up_ref, down_ref, rows_ref, act_ref, sems,
):
    chunk_rows, wide = x_ref.shape
    block = wide // BLOCKS
    half = gate_a.shape[1]
    low, high = slice(0, half), slice(half, 2 * half)
    cuts = 4
    deep = gate_a.shape[0] // cuts
    steps = [slice(i * deep, (i + 1) * deep) for i in range(cuts)]
    parts = [
        start(
            (gate_a.at[k], gate_ref.at[k, low], sems.at[4 * i]),
            (gate_b.at[k], gate_ref.at[k, high], sems.at[4 * i + 1]),
            (up_a.at[k], up_ref.at[k, low], sems.at[4 * i + 2]),
            (up_b.at[k], up_ref.at[k, high], sems.at[4 * i + 3]),
        )
        for i, k in enumerate(steps)
    ]
    downs = start(
        (down_a, down_ref.at[low], sems.at[4 * cuts]),
        (down_b, down_ref.at[high], sems.at[4 * cuts + 1]),
    )

    step = 256
    chunks = step // GROUP
    packed = chunks * CAP

    def onehot(t, c):
        return ((c // GROUP == t % chunks) & (c % GROUP == t // chunks)).astype(F32).astype(BF16)

    gather = onehot(iota((step, step), 0), iota((step, step), 1))
    spread = onehot(iota((step, step), 1), iota((step, step), 0))
    groups = range(chunk_rows // step)
    for g in groups:
        for j in range(BLOCKS):
            at = slice(j * block, (j + 1) * block)
            moved = dot(gather, x_ref[g * step : (g + 1) * step, at]).astype(BF16)
            rows_ref[g * packed : (g + 1) * packed, at] = moved[:packed]
            for i, k in enumerate((j, BLOCKS + j)):
                target = g * packed + k * chunks
                rows_ref[target : target + chunks, wide:] = moved[packed + i * chunks :][:chunks]

    gate = up = 0.0
    for k, copies in zip(steps, parts):
        finish(copies)
        gate = gate + dot(rows_ref[:, k], gate_ref[k])
        up = up + dot(rows_ref[:, k], up_ref[k])
    act_ref[...] = (gate / (1.0 + jnp.exp(-gate)) * up).astype(BF16)
    finish(downs)
    last = dot(act_ref[...], down_ref[:, wide:]).astype(BF16)
    for j in range(BLOCKS):
        at = slice(j * block, (j + 1) * block)
        result = dot(act_ref[...], down_ref[:, at]).astype(BF16)
        for g in groups:
            source, target = g * packed, slice(g * step, (g + 1) * step)
            tails = [source + (j + k) * chunks for k in (0, BLOCKS)]
            both = [result[source : source + packed]] + [last[i : i + chunks] for i in tails]
            out_ref[target, at] = dot(spread, jnp.concatenate(both, axis=0)).astype(BF16)


def places_kernel(routes_ref, scale_ref, at_ref, share_ref):
    length = routes_ref.shape[0]
    scale = scale_ref[...]
    share_ref[...] = scale / jnp.sum(scale, axis=1, keepdims=True)
    expert = iota((length, 128), 1)
    hits = [expert == routes_ref[:, r : r + 1] for r in range(2)]
    named = (hits[0] | hits[1]).astype(F32).astype(BF16)
    earlier = (iota((length, length), 1) < iota((length, length), 0)).astype(F32).astype(BF16)
    position = dot(earlier, named)
    for r in range(2):
        k = jnp.sum(jnp.where(hits[r], position, 0.0), axis=1, keepdims=True).astype(I32)
        at_ref[:, r : r + 1] = routes_ref[:, r : r + 1] * GROUP + k


def combine_kernel(at_ref, share_ref, back_ref, out_hbm, out_ref, sems):
    length = at_ref.shape[0]
    slots = back_ref.shape[0]
    block = back_ref.shape[1] // BLOCKS
    share = share_ref[...]
    slot = iota((length, slots), 1)
    places = [at_ref[:, r : r + 1] for r in range(2)]

    def onehot(index):
        return (slot == index).astype(F32).astype(BF16)

    main = [onehot(place) for place in places]
    tails = [jnp.zeros((length, block), F32) for _ in range(2)]
    copies = []
    for j in range(BLOCKS):
        at = slice(j * block, (j + 1) * block)
        picks = list(main)
        for place in places:
            k, base = place % GROUP, place - place % GROUP
            second = k >= BLOCKS
            mine = jnp.where(second, k - BLOCKS, k) == j
            picks.append(onehot(jnp.where(mine, base + CAP + second.astype(I32), -1)))
        got = dot(jnp.concatenate(picks, axis=0), back_ref[:, at])
        total = share[:, 0:1] * got[:length] + share[:, 1:2] * got[length : 2 * length]
        out_ref[:, at] = total.astype(BF16)
        copies += start((out_ref.at[:, at], out_hbm.at[:, at], sems.at[j]))
        for r in range(2):
            tails[r] = tails[r] + got[(2 + r) * length : (3 + r) * length]
    total = share[:, 0:1] * tails[0] + share[:, 1:2] * tails[1]
    at = slice(BLOCKS * block, (BLOCKS + 1) * block)
    out_ref[:, at] = total.astype(BF16)
    finish(copies + start((out_ref.at[:, at], out_hbm.at[:, at], sems.at[BLOCKS])))


def call(kernel, out, *args, flops, scratch, sems, here=(), out_here=False, limit=32 << 20):
    moved = sum(a.size * a.dtype.itemsize for a in args) + out[0] * out[1] * 2
    return pl.pallas_call(
        kernel,
        out_shape=jax.ShapeDtypeStruct(out, BF16),
        in_specs=[VMEM if i in here else ANY for i in range(len(args))],
        out_specs=VMEM if out_here else ANY,
        scratch_shapes=[pltpu.VMEM(*s) for s in scratch] + [pltpu.SemaphoreType.DMA((sems,))],
        compiler_params=pltpu.CompilerParams(vmem_limit_bytes=limit),
        cost_estimate=pl.CostEstimate(flops=flops, bytes_accessed=moved, transcendentals=0),
    )(*args)


def pack(counts, owner, rows, length):
    width = rows.shape[1]
    return call(
        pack_kernel, (length, width), counts, owner, rows,
        flops=2 * length * rows.shape[0] * width,
        scratch=[
            (counts.shape, I32), (owner.shape, I32), (rows.shape, BF16), ((length, width), BF16),
        ],
        sems=4, limit=62 << 20,
    )


def find_slots(routes_t, slots):
    return pl.pallas_call(
        slots_kernel,
        out_shape=jax.ShapeDtypeStruct((slots, (BLOCKS + 1) * routes_t.shape[1]), BF16),
        compiler_params=pltpu.CompilerParams(vmem_limit_bytes=16 << 20),
    )(routes_t)


def dispatch(picks, sequence, wide):
    length, slots = sequence.shape[0], picks.shape[0]
    return call(
        dispatch_kernel, (slots, wide), picks, sequence,
        flops=4 * slots * length * wide,
        scratch=[((slots, wide), BF16)], sems=BLOCKS, here=(0, 1),
    )


def run_expert(received, own, other):
    slots, wide = received.shape
    width, half = own[0].shape
    rows = slots // GROUP * CAP
    return call(
        expert_kernel, (slots, wide), received, *own, *other,
        flops=12 * slots * width * half,
        scratch=[
            ((width, 2 * half), BF16), ((width, 2 * half), BF16), ((2 * half, width), BF16),
            ((rows, width), BF16), ((rows, 2 * half), BF16),
        ],
        sems=18, here=(0,), out_here=True, limit=48 << 20,
    )


def find_places(routes, route_scale):
    return pl.pallas_call(
        places_kernel,
        out_shape=[
            jax.ShapeDtypeStruct(routes.shape, I32),
            jax.ShapeDtypeStruct(routes.shape, F32),
        ],
        compiler_params=pltpu.CompilerParams(vmem_limit_bytes=16 << 20),
    )(routes, route_scale)


def combine(at, share, returned, width):
    length, slots = at.shape[0], returned.shape[0]
    return call(
        combine_kernel, (length, width), at, share, returned,
        flops=8 * length * slots * returned.shape[1],
        scratch=[((length, width), BF16)], sems=BLOCKS + 1, here=(0, 1, 2),
    )


def local(image_rows, image_counts, image_owner, routes, route_scale, w_gate, w_up, w_down):
    owners = lax.axis_size(("dp", "mp"))
    experts = lax.axis_size("expert")
    length = routes.shape[0]
    width = image_rows.shape[1]
    slots = experts * GROUP
    wide = width // (BLOCKS + 1) * BLOCKS
    own = [w_gate[0], w_up[0], w_down[0]]
    other = [lax.ppermute(w, "mp", [(0, 1), (1, 0)]) for w in own]

    outgoing = pack(image_counts, image_owner, image_rows, length)
    arrived = lax.all_to_all(
        outgoing.reshape(owners, length // owners, width),
        ("dp", "mp"),
        split_axis=0,
        concat_axis=0,
        tiled=True,
    )
    picks = find_slots(routes.T, slots)
    buffer = dispatch(picks, arrived.reshape(length, width), wide)

    def exchange(x):
        y = lax.all_to_all(
            x.reshape(experts, GROUP, wide), "expert", split_axis=0, concat_axis=0, tiled=True
        )
        return y.reshape(slots, wide)

    received = exchange(buffer)
    received, places = lax.optimization_barrier((received, find_places(routes, route_scale)))
    returned = exchange(run_expert(received, own, other))
    return combine(*places, returned, width)


def solution(mesh):
    return jax.shard_map(
        local,
        mesh=mesh,
        in_specs=(
            P(("dp", "expert", "mp"), None),
            P(("dp", "expert", "mp"), None),
            P(("dp", "expert", "mp"), None),
            P(("dp", "expert", "mp"), None),
            P(("dp", "expert", "mp"), None),
            P("expert", None, "mp"),
            P("expert", None, "mp"),
            P("expert", "mp", None),
        ),
        out_specs=P(("dp", "expert", "mp"), None),
        check_vma=False,
    )
```
